32 devices in a mesh: space: 16 (over z, x, core), hist: 2 (over y).
Axes of the slice: x: 2, y: 2, z: 4, core: 2. Of those that a mesh axis runs over, the one named last changes fastest.
Arguments:
- history: bfloat16 [8, 64, 8192], P('hist', None, 'space'), may hold values from -6 to 6
- right_factor: bfloat16 [64, 80, 8192], P('hist', None, 'space'), may hold values from -0.25 to 0.25
- left_factor: bfloat16 [64, 80, 8192], P('hist', None, 'space'), may hold values from -0.25 to 0.25
- pair_rank: int32 [64, 16], P('hist', 'space'), may hold values from 20 to 80
- pair_lag: int32 [64, 16], P('hist', 'space'), may hold values from 0 to 3
- near_block: bfloat16 [3, 8192, 512], P(None, 'space'), may hold values from -0.09695897 to 0.09695897, as said below
- self_term: float32 [8192], P('space'), may hold values from 1 to 1.5
- excitation: float32 [64, 8192], P(None, 'space'), may hold values from -6 to 6
Outputs:
- new_current: float32 [64, 8192], P(None, 'space')
- next_history: bfloat16 [8, 64, 8192], P('hist', None, 'space')
The draws below stay inside these ranges and needn't reach their ends.
Inputs may be any that keep to these rules, and one draw needn't show every extreme that they name: Entries of near_block lie within 3.8 times (1536) to the power -0.5 in magnitude.
All inputs are finite; a program needn't handle non-finite values.
Results may differ from the reference program's by a relative error of at most 0.015.
Values may be sent and summed in bfloat16 or wider, within the bound.
A program may use at most 64 MiB of HBM per device.

```python
import jax
import jax.numpy as jnp
from jax import lax

B_DEV = 512
K = 64
RMAX = 80
PPT = 2
LAG_DEV = 4
SWEEPS = 8
N = 8192
PAIR_DEV = 32
NPAIRS = 64
LAGS = 8
N_SPACE = 16
N_HIST = 2


def draw_near_block(key, part):
    spread = 0.95 * (3.0 * B_DEV) ** (-0.5)
    inner = jax.random.fold_in(key, 7301)
    values = jnp.clip(jax.random.normal(inner, (3, N, B_DEV), jnp.float32), -4.0, 4.0) * spread
    values = jnp.clip(values, -3.7 * (3.0 * B_DEV) ** (-0.5), 3.7 * (3.0 * B_DEV) ** (-0.5))
    return values.astype(jnp.bfloat16)


def touch_ends(entries, own_key, low, largest):
    shape = entries.shape
    index_at = [jax.random.randint(jax.random.fold_in(own_key, axis), (), 0, shape[axis]) for axis in range(len(shape))]
    entries = entries.at[tuple(index_at)].set(low)
    longest = shape.index(max(shape))
    index_at[longest] = (index_at[longest] + 1) % shape[longest]
    return entries.at[tuple(index_at)].set(largest)


def block_levels(key, extent, cuts, low, top_value):
    factor_of = 1.0
    for dim, shards_of in cuts:
        steps = jax.random.uniform(jax.random.fold_in(jax.random.fold_in(key, 6), dim), (shards_of,), jnp.float32, low / len(cuts), top_value / len(cuts))
        factor_of = factor_of * jnp.repeat(jnp.exp(steps), extent[dim] // shards_of).reshape((-1,) + (1,) * (len(extent) - 1 - dim))
    return factor_of


def centred(own_key, dims, scale, reach, shards=(), kind=jnp.bfloat16):
    values = jax.random.normal(own_key, dims, jnp.float32) * scale
    if len(shards) > 0:
        values = block_levels(own_key, dims, shards, -0.22, 0.18) * values
    return jnp.clip(values, min=-reach, max=reach).astype(kind)


def setup_inputs(seed: int = 0) -> dict:
    key_list = jax.random.split(jax.random.key(seed), 9)
    history = centred(key_list[0], (LAGS, K, N), 1.0, 6.0, ((0, 2), (2, 16)))
    right_factor = centred(key_list[1], (NPAIRS, RMAX, N), B_DEV ** -0.5, 0.25, ((0, 2), (2, 16)))
    left_factor = centred(key_list[2], (NPAIRS, RMAX, N), (RMAX * PPT * N_HIST * 2) ** -0.5, 0.25, ((0, 2), (2, 16)))
    pair_rank = touch_ends(jax.random.randint(key_list[3], (NPAIRS, N_SPACE), RMAX // 4, RMAX + 1), jax.random.fold_in(key_list[3], 1), RMAX // 4, RMAX).astype(jnp.int32)
    pair_lag = touch_ends(jax.random.randint(key_list[4], (NPAIRS, N_SPACE), 0, LAG_DEV), jax.random.fold_in(key_list[4], 1), 0, LAG_DEV - 1).astype(jnp.int32)
    near_block = draw_near_block(jax.random.fold_in(key_list[8], 71), 0)
    self_term = jnp.clip(1.0 + 0.5 * jax.random.uniform(key_list[6], (N,), jnp.float32) ** block_levels(key_list[6], (N,), ((0, 16),), -0.2, 0.2), 1.0, 1.5)
    excitation = centred(key_list[7], (K, N), 1.0, 6.0, ((1, 16),), jnp.float32)
    return {"history": history, "right_factor": right_factor, "left_factor": left_factor, "pair_rank": pair_rank, "pair_lag": pair_lag, "near_block": near_block, "self_term": self_term, "excitation": excitation}


def reference(history, right_factor, left_factor, pair_rank, pair_lag, near_block, self_term, excitation):
    total = N_SPACE * B_DEV
    pair_count = PAIR_DEV * N_HIST
    group_base = (jnp.arange(pair_count, dtype=jnp.int32) // PAIR_DEV) * LAG_DEV
    levels = jnp.arange(RMAX, dtype=jnp.int32)

    def add_source(source, accum):
        source = jnp.asarray(source).astype(jnp.int32)
        start = (source * B_DEV).astype(jnp.int32)
        right_cols = lax.dynamic_slice_in_dim(right_factor, start, B_DEV, 2)
        left_cols = lax.dynamic_slice_in_dim(left_factor, start, B_DEV, 2)
        hist_cols = lax.dynamic_slice_in_dim(history, start, B_DEV, 2)
        lag_column = lax.dynamic_index_in_dim(pair_lag, source, 1, keepdims=False).astype(jnp.int32)
        ranks = lax.dynamic_index_in_dim(pair_rank, source, 1, keepdims=False)
        chosen = jnp.take(hist_cols, group_base + lag_column, axis=0)
        coefficient = jnp.einsum("prb,pkb->prk", right_cols.astype(jnp.float32), chosen.astype(jnp.float32))
        coefficient = jnp.where(levels[None, :, None] < ranks[:, None, None], coefficient, 0.0).astype(jnp.bfloat16)
        coefficient = coefficient.reshape(N_HIST, N_SPACE, PPT * RMAX, K).astype(jnp.float32)
        left_rows = left_cols.reshape(N_HIST, N_SPACE, PPT * RMAX, B_DEV).astype(jnp.float32)
        return accum + jnp.einsum("htck,htcb->tkb", coefficient, left_rows)

    far_field = lax.fori_loop(0, N_SPACE, add_source, jnp.zeros((N_SPACE, K, B_DEV), jnp.float32))
    far_field = far_field.transpose(1, 0, 2).reshape(K, total)
    right_side = excitation - far_field
    blocks = near_block.astype(jnp.float32).reshape(3, N_SPACE, B_DEV, B_DEV)

    def near_apply(current):
        rounded = lax.optimization_barrier(current.astype(jnp.bfloat16)).astype(jnp.float32)
        padded = jnp.pad(rounded, ((0, 0), (B_DEV, B_DEV)))
        product = self_term[None, :] * current
        for offset in range(3):
            beside = padded[:, offset * B_DEV: offset * B_DEV + total].reshape(K, N_SPACE, B_DEV)
            product = product + jnp.einsum("ktj,tij->kti", beside, blocks[offset]).reshape(K, total)
        return product

    current = jnp.zeros((K, total), jnp.float32)
    for sweep_index in range(SWEEPS):
        current = current + (right_side - near_apply(current)) / self_term[None, :]
    newest = current.astype(jnp.bfloat16)
    next_history = jnp.concatenate([newest[None], history[:-1]], axis=0)
    return current, next_history
```

```python
import functools

import jax
import jax.numpy as jnp
from jax import lax
from jax.experimental import pallas as pl
from jax.experimental.pallas import tpu as pltpu
from jax.sharding import PartitionSpec as P

SWEEPS = 8
MESH = pl.DeviceIdType.MESH
NT = (((1,), (1,)), ((), ()))


def shape_of(space):
    cores = 2
    chips = space // cores
    z_size = 1
    while z_size * z_size * 4 <= space and chips % (z_size * 2) == 0:
        z_size *= 2
    return z_size, chips // z_size, cores


def kernel(
    dims,
    lag_ref, rank_ref, hist_ref, self_ref, exc_ref, right_hbm, left_hbm, near_hbm,
    cur_out, hist_out,
    rbuf, lbuf, nbuf, p1, r1, q, r2, t3, r3, xs, halo, xlast, gath, hin,
    rsem, lsem, nsem, s1s, s1r, s2s, s2r, s3s, s3r, xss, xsr, gs, gr, hs,
):
    space, hists, z_size, x_size, per, rank_most = dims
    lags, steps, width = hist_ref.shape
    kh = steps // hists
    me = lax.axis_index("space")
    h = lax.axis_index("hist")
    core = lax.rem(me, 2)
    chip = me // 2
    x = lax.rem(chip, x_size)
    z = chip // x_size
    mate = me + 1 - 2 * core
    half = space // 2
    group = x_size * hists
    slot = x * hists + h

    def chip_at(j):
        zo, xo = j // x_size, lax.rem(j, x_size)
        zt = lax.rem(z + 1 + zo, z_size)
        xt = lax.rem(x + 1 + xo, x_size)
        return zt, xt

    def load(t):
        rows = pl.ds(t * per, per)
        return (
            pltpu.make_async_copy(right_hbm.at[rows], rbuf.at[rows], rsem.at[t]),
            pltpu.make_async_copy(left_hbm.at[rows], lbuf.at[rows], lsem.at[t]),
        )

    def space_id(zt, xt):
        return (zt * x_size + xt) * 2 + core

    barrier = pltpu.get_barrier_semaphore()

    def greet(s, hh):
        pl.semaphore_signal(barrier, inc=1, device_id=(s, hh), device_id_type=MESH)

    greet(mate, h)
    for o in range(1, group):
        sl = lax.rem(slot + o, group)
        greet(space_id(z, sl // hists), lax.rem(sl, hists))
    for o in range(1, z_size):
        greet(space_id(lax.rem(z + o, z_size), x), h)

    @pl.when(me > 0)
    def _():
        greet(me - 1, h)

    @pl.when(me < space - 1)
    def _():
        greet(me + 1, h)

    for side in range(2):
        def start(j, carry):
            zt, xt = chip_at(j)
            own = core if side else 1 - core
            for c in load((zt * x_size + xt) * 2 + own):
                c.start()
            return carry

        lax.fori_loop(0, half, start, 0)
    near_copy = pltpu.make_async_copy(near_hbm, nbuf, nsem)
    near_copy.start()

    hist_all = hist_ref[...].reshape(lags * steps, width)
    cols = lax.broadcasted_iota(jnp.int32, (1, per * rank_most), 1)

    def partial_of(t):
        for c in load(t):
            c.wait()
        rows = pl.ds(t * per, per)
        rr = rbuf[rows].reshape(per * rank_most, width)
        ll = lbuf[rows].reshape(per * rank_most, width)
        lag = jnp.full(cols.shape, lag_ref[t * per], jnp.int32)
        lim = jnp.full(cols.shape, rank_ref[t * per], jnp.int32)
        for i in range(1, per):
            at = cols >= i * rank_most
            lag = jnp.where(at, lag_ref[t * per + i], lag)
            lim = jnp.where(at, rank_ref[t * per + i] + i * rank_most, lim)
        lag = jnp.where(cols < lim, lag, lags)
        full = lax.dot_general(hist_all, rr, NT, preferred_element_type=jnp.float32)
        coef = jnp.zeros((steps, per * rank_most), jnp.float32)
        for g in range(lags):
            coef = jnp.where(lag == g, full[g * steps : (g + 1) * steps], coef)
        return jnp.dot(coef.astype(jnp.bfloat16), ll, preferred_element_type=jnp.float32)

    def copy1(b):
        return pltpu.make_async_remote_copy(
            src_ref=p1.at[b], dst_ref=r1.at[b], send_sem=s1s.at[b], recv_sem=s1r.at[b],
            device_id=(mate, h), device_id_type=MESH,
        )

    ends = jnp.minimum(me, 1) + jnp.minimum(space - 1 - me, 1)
    pl.semaphore_wait(barrier, 1 + (group - 1) + (z_size - 1) + ends)

    hist_copy = pltpu.make_async_remote_copy(
        src_ref=hist_ref.at[lags - 1], dst_ref=hin, send_sem=hs.at[0], recv_sem=hs.at[1],
        device_id=(me, lax.rem(h + 1, hists)), device_id_type=MESH,
    )

    def first(j, carry):
        zt, xt = chip_at(j)
        b = zt * x_size + xt
        p1[b] = partial_of(b * 2 + 1 - core).astype(jnp.bfloat16)
        copy1(b).start()
        return carry

    lax.fori_loop(0, half, first, 0)

    def copy2(zt, xt, ht):
        return pltpu.make_async_remote_copy(
            src_ref=q.at[zt, xt * hists + ht], dst_ref=r2.at[zt, slot],
            send_sem=s2s.at[zt, xt * hists + ht], recv_sem=s2r.at[zt, slot],
            device_id=(space_id(z, xt), ht), device_id_type=MESH,
        )

    def second(j, carry):
        zt, xt = chip_at(j)
        b = zt * x_size + xt
        value = partial_of(b * 2 + core)
        copy1(b).wait_recv()
        value = value + r1[b].astype(jnp.float32)
        low = value.astype(jnp.bfloat16)
        for ht in range(hists):
            part = low[ht * kh : (ht + 1) * kh]
            mine = jnp.logical_and(xt == x, h == ht)

            @pl.when(mine)
            def _():
                r2[zt, slot] = part

            @pl.when(jnp.logical_not(mine))
            def _():
                q[zt, xt * hists + ht] = part
                copy2(zt, xt, ht).start()
        return carry

    lax.fori_loop(0, half, second, 0)
    hist_copy.start()

    def gather2(zt):
        def wait(o, carry):
            sl = lax.rem(slot + o, group)
            pltpu.make_async_remote_copy(
                src_ref=q.at[zt, sl], dst_ref=r2.at[zt, sl],
                send_sem=s2s.at[zt, sl], recv_sem=s2r.at[zt, sl],
                device_id=(space_id(z, sl // hists), lax.rem(sl, hists)), device_id_type=MESH,
            ).wait_recv()
            return carry

        lax.fori_loop(1, group, wait, 0)
        return jnp.sum(r2[zt].astype(jnp.float32), axis=0)

    def copy3(zt):
        return pltpu.make_async_remote_copy(
            src_ref=t3.at[zt], dst_ref=r3.at[z], send_sem=s3s.at[zt], recv_sem=s3r.at[z],
            device_id=(space_id(zt, x), h), device_id_type=MESH,
        )

    def third(zo, carry):
        zt = lax.rem(z + 1 + zo, z_size)
        t3[zt] = gather2(zt).astype(jnp.bfloat16)
        copy3(zt).start()
        return carry

    lax.fori_loop(0, z_size - 1, third, 0)
    far = gather2(z)

    inverse = 1.0 / self_ref[...]
    for l in range(1, lags):
        hist_out[l] = hist_ref[l - 1]

    @pl.when(me == 0)
    def _():
        for n in range(SWEEPS - 1):
            halo[n, 0] = jnp.zeros((kh, width), jnp.bfloat16)

    @pl.when(me == space - 1)
    def _():
        for n in range(SWEEPS - 1):
            halo[n, 1] = jnp.zeros((kh, width), jnp.bfloat16)

    for o in range(1, z_size):
        zs = lax.rem(z + o, z_size)
        pltpu.make_async_remote_copy(
            src_ref=t3.at[zs], dst_ref=r3.at[zs], send_sem=s3s.at[zs], recv_sem=s3r.at[zs],
            device_id=(space_id(zs, x), h), device_id_type=MESH,
        ).wait_recv()
        far = far + r3[zs].astype(jnp.float32)
    near_copy.wait()
    right_side = exc_ref[h] - far
    current = right_side * inverse

    def edge(n, side):
        other = jnp.minimum(me + 1, space - 1) if side == 0 else jnp.maximum(me - 1, 0)
        return pltpu.make_async_remote_copy(
            src_ref=xs.at[n], dst_ref=halo.at[n, side],
            send_sem=xss.at[n, side], recv_sem=xsr.at[n, side],
            device_id=(other, h), device_id_type=MESH,
        )

    for n in range(SWEEPS - 1):
        rounded = current.astype(jnp.bfloat16)
        xs[n] = rounded

        @pl.when(me < space - 1)
        def _():
            edge(n, 0).start()

        @pl.when(me > 0)
        def _():
            edge(n, 1).start()

        product = lax.dot_general(rounded, nbuf[1], NT, preferred_element_type=jnp.float32)
        rest = right_side - product

        @pl.when(me > 0)
        def _():
            edge(n, 0).wait_recv()

        @pl.when(me < space - 1)
        def _():
            edge(n, 1).wait_recv()

        before = lax.dot_general(halo[n, 0], nbuf[0], NT, preferred_element_type=jnp.float32)
        after = lax.dot_general(halo[n, 1], nbuf[2], NT, preferred_element_type=jnp.float32)
        current = (rest - before - after) * inverse

    xlast[...] = current

    def give(o):
        ht = lax.rem(h + o, hists)
        return pltpu.make_async_remote_copy(
            src_ref=xlast, dst_ref=gath.at[h], send_sem=gs.at[ht], recv_sem=gr.at[h],
            device_id=(me, ht), device_id_type=MESH,
        )

    for o in range(1, hists):
        give(o).start()
    cur_out[h] = current
    hist_copy.wait()

    def drain(j, carry):
        zt, xt = chip_at(j)
        copy1(zt * x_size + xt).wait_send()
        for ht in range(hists):
            @pl.when(jnp.logical_not(jnp.logical_and(xt == x, h == ht)))
            def _():
                copy2(zt, xt, ht).wait_send()
        return carry

    lax.fori_loop(0, half, drain, 0)
    for o in range(1, z_size):
        copy3(lax.rem(z + o, z_size)).wait_send()

    @pl.when(me < space - 1)
    def _():
        for n in range(SWEEPS - 1):
            edge(n, 0).wait_send()

    @pl.when(me > 0)
    def _():
        for n in range(SWEEPS - 1):
            edge(n, 1).wait_send()

    for o in range(1, hists):
        hs_ = lax.rem(h + o, hists)
        pltpu.make_async_remote_copy(
            src_ref=xlast, dst_ref=gath.at[hs_], send_sem=gs.at[hs_], recv_sem=gr.at[hs_],
            device_id=(me, hs_), device_id_type=MESH,
        ).wait_recv()
        cur_out[hs_] = gath[hs_]
    for o in range(1, hists):
        give(o).wait_send()

    @pl.when(h == 0)
    def _():
        hist_out[0] = cur_out[...].reshape(steps, width).astype(jnp.bfloat16)

    @pl.when(h > 0)
    def _():
        hist_out[0] = hin[...]


def per_device(
    space, hists,
    history, right_factor, left_factor, pair_rank, pair_lag, near_block, self_term, excitation,
):
    lags, steps, width = history.shape
    pair_dev, rank_most, _ = right_factor.shape
    z_size, x_size, _ = shape_of(space)
    per = pair_dev // space
    kh = steps // hists
    half, group = space // 2, x_size * hists
    sweeps = SWEEPS - 1
    bf16 = jnp.bfloat16
    dma = pltpu.SemaphoreType.DMA
    vmem = pl.BlockSpec(memory_space=pltpu.VMEM)
    smem = pl.BlockSpec(memory_space=pltpu.SMEM)
    any_ = pl.BlockSpec(memory_space=pl.ANY)
    flops = 2 * pair_dev * rank_most * width * steps * 2
    current, next_history = pl.pallas_call(
        functools.partial(kernel, (space, hists, z_size, x_size, per, rank_most)),
        out_shape=(
            jax.ShapeDtypeStruct((hists, kh, width), jnp.float32),
            jax.ShapeDtypeStruct((lags, steps, width), bf16),
        ),
        in_specs=[smem, smem, vmem, vmem, vmem, any_, any_, any_],
        out_specs=(vmem, vmem),
        scratch_shapes=[
            pltpu.VMEM((pair_dev, rank_most, width), bf16),
            pltpu.VMEM((pair_dev, rank_most, width), bf16),
            pltpu.VMEM(near_block.shape, bf16),
            pltpu.VMEM((half, steps, width), bf16),
            pltpu.VMEM((half, steps, width), bf16),
            pltpu.VMEM((z_size, group, kh, width), bf16),
            pltpu.VMEM((z_size, group, kh, width), bf16),
            pltpu.VMEM((z_size, kh, width), bf16),
            pltpu.VMEM((z_size, kh, width), bf16),
            pltpu.VMEM((sweeps, kh, width), bf16),
            pltpu.VMEM((sweeps, 2, kh, width), bf16),
            pltpu.VMEM((kh, width), jnp.float32),
            pltpu.VMEM((hists, kh, width), jnp.float32),
            pltpu.VMEM((steps, width), bf16),
            dma((space,)), dma((space,)), dma,
            dma((half,)), dma((half,)),
            dma((z_size, group)), dma((z_size, group)),
            dma((z_size,)), dma((z_size,)),
            dma((sweeps, 2)), dma((sweeps, 2)),
            dma((hists,)), dma((hists,)), dma((2,)),
        ],
        compiler_params=pltpu.CompilerParams(
            collective_id=0, has_side_effects=True, vmem_limit_bytes=48 * 1024 * 1024
        ),
        cost_estimate=pl.CostEstimate(
            flops=flops, bytes_accessed=4 * pair_dev * rank_most * width, transcendentals=0
        ),
    )(
        pair_lag.reshape(-1), pair_rank.reshape(-1), history, self_term.reshape(1, width),
        excitation.reshape(hists, kh, width), right_factor, left_factor, near_block,
    )
    return current.reshape(steps, width), next_history


def solution(mesh):
    in_specs = (
        P("hist", None, "space"),
        P("hist", None, "space"),
        P("hist", None, "space"),
        P("hist", "space"),
        P("hist", "space"),
        P(None, "space", None),
        P("space"),
        P(None, "space"),
    )
    out_specs = (P(None, "space"), P("hist", None, "space"))
    step = functools.partial(per_device, mesh.shape["space"], mesh.shape["hist"])
    return jax.shard_map(
        step, mesh=mesh, in_specs=in_specs, out_specs=out_specs, check_vma=False
    )
```

```python
import functools

import jax
import jax.numpy as jnp
from jax import lax
from jax.experimental import pallas as pl
from jax.experimental.pallas import tpu as pltpu
from jax.sharding import PartitionSpec as P

SWEEPS = 8
MESH = pl.DeviceIdType.MESH
NT = (((1,), (1,)), ((), ()))


def shape_of(space):
    cores = 2
    chips = space // cores
    z_size = 1
    while z_size * z_size * 4 <= space and chips % (z_size * 2) == 0:
        z_size *= 2
    return z_size, chips // z_size, cores


def kernel(
    dims,
    lag_hbm, rank_hbm, hist_hbm, self_hbm, exc_hbm, right_hbm, left_hbm, near_hbm,
    cur_hbm, hist_hbm_out,
    lag_ref, rank_ref, hist_ref, self_ref, exc_ref, cur_out, newest, rbuf, lbuf, nbuf, p1, r1, q, r2, t3, r3, xs, halo, xlast, gath, hin,
    rsem, lsem, nsem, s1s, s1r, s2s, s2r, s3s, s3r, xss, xsr, gs, gr, hs, isem, osem,
):
    space, hists, z_size, x_size, per, rank_most = dims
    lags, steps, width = hist_ref.shape
    kh = steps // hists
    me = lax.axis_index("space")
    h = lax.axis_index("hist")
    core = lax.rem(me, 2)
    chip = me // 2
    x = lax.rem(chip, x_size)
    z = chip // x_size
    mate = me + 1 - 2 * core
    half = space // 2
    group = x_size * hists
    slot = x * hists + h

    def chip_at(j):
        zo, xo = j // x_size, lax.rem(j, x_size)
        zt = lax.rem(z + 1 + zo, z_size)
        xt = lax.rem(x + 1 + xo, x_size)
        return zt, xt

    def load(t):
        rows = pl.ds(t * per, per)
        return (
            pltpu.make_async_copy(right_hbm.at[rows], rbuf.at[rows], rsem.at[t]),
            pltpu.make_async_copy(left_hbm.at[rows], lbuf.at[rows], lsem.at[t]),
        )

    def space_id(zt, xt):
        return (zt * x_size + xt) * 2 + core

    inputs = [
        pltpu.make_async_copy(a, b, isem.at[i])
        for i, (a, b) in enumerate((
            (hist_hbm, hist_ref), (lag_hbm, lag_ref), (rank_hbm, rank_ref),
            (exc_hbm.at[h], exc_ref), (self_hbm, self_ref),
        ))
    ]
    shift = pltpu.make_async_copy(
        hist_hbm.at[pl.ds(0, lags - 1)], hist_hbm_out.at[pl.ds(1, lags - 1)], osem.at[2]
    )
    for c in inputs[:3]:
        c.start()

    barrier = pltpu.get_barrier_semaphore()

    def greet(s, hh):
        pl.semaphore_signal(barrier, inc=1, device_id=(s, hh), device_id_type=MESH)

    greet(mate, h)
    for o in range(1, group):
        sl = lax.rem(slot + o, group)
        greet(space_id(z, sl // hists), lax.rem(sl, hists))
    for o in range(1, z_size):
        greet(space_id(lax.rem(z + o, z_size), x), h)

    @pl.when(me > 0)
    def _():
        greet(me - 1, h)

    @pl.when(me < space - 1)
    def _():
        greet(me + 1, h)

    for side in range(2):
        def start(j, carry):
            zt, xt = chip_at(j)
            own = core if side else 1 - core
            for c in load((zt * x_size + xt) * 2 + own):
                c.start()
            return carry

        lax.fori_loop(0, half, start, 0)
    near_copy = pltpu.make_async_copy(near_hbm, nbuf, nsem)
    near_copy.start()
    inputs[3].start()
    inputs[4].start()
    shift.start()

    for c in inputs[:3]:
        c.wait()
    hist_all = hist_ref[...].reshape(lags * steps, width)
    cols = lax.broadcasted_iota(jnp.int32, (1, per * rank_most), 1)

    def partial_of(t):
        for c in load(t):
            c.wait()
        rows = pl.ds(t * per, per)
        rr = rbuf[rows].reshape(per * rank_most, width)
        ll = lbuf[rows].reshape(per * rank_most, width)
        lag = jnp.full(cols.shape, lag_ref[t * per], jnp.int32)
        lim = jnp.full(cols.shape, rank_ref[t * per], jnp.int32)
        for i in range(1, per):
            at = cols >= i * rank_most
            lag = jnp.where(at, lag_ref[t * per + i], lag)
            lim = jnp.where(at, rank_ref[t * per + i] + i * rank_most, lim)
        lag = jnp.where(cols < lim, lag, lags)
        full = lax.dot_general(hist_all, rr, NT, preferred_element_type=jnp.float32)
        coef = jnp.zeros((steps, per * rank_most), jnp.float32)
        for g in range(lags):
            coef = jnp.where(lag == g, full[g * steps : (g + 1) * steps], coef)
        return jnp.dot(coef.astype(jnp.bfloat16), ll, preferred_element_type=jnp.float32)

    def copy1(b):
        return pltpu.make_async_remote_copy(
            src_ref=p1.at[b], dst_ref=r1.at[b], send_sem=s1s.at[b], recv_sem=s1r.at[b],
            device_id=(mate, h), device_id_type=MESH,
        )

    ends = jnp.minimum(me, 1) + jnp.minimum(space - 1 - me, 1)
    pl.semaphore_wait(barrier, 1 + (group - 1) + (z_size - 1) + ends)

    hist_copy = pltpu.make_async_remote_copy(
        src_ref=hist_ref.at[lags - 1], dst_ref=hin, send_sem=hs.at[0], recv_sem=hs.at[1],
        device_id=(me, lax.rem(h + 1, hists)), device_id_type=MESH,
    )

    def first(j, carry):
        zt, xt = chip_at(j)
        b = zt * x_size + xt
        p1[b] = partial_of(b * 2 + 1 - core).astype(jnp.bfloat16)
        copy1(b).start()
        return carry

    lax.fori_loop(0, half, first, 0)

    def copy2(zt, xt, ht):
        return pltpu.make_async_remote_copy(
            src_ref=q.at[zt, xt * hists + ht], dst_ref=r2.at[zt, slot],
            send_sem=s2s.at[zt, xt * hists + ht], recv_sem=s2r.at[zt, slot],
            device_id=(space_id(z, xt), ht), device_id_type=MESH,
        )

    def second(j, carry):
        zt, xt = chip_at(j)
        b = zt * x_size + xt
        value = partial_of(b * 2 + core)
        copy1(b).wait_recv()
        value = value + r1[b].astype(jnp.float32)
        low = value.astype(jnp.bfloat16)
        for ht in range(hists):
            part = low[ht * kh : (ht + 1) * kh]
            mine = jnp.logical_and(xt == x, h == ht)

            @pl.when(mine)
            def _():
                r2[zt, slot] = part

            @pl.when(jnp.logical_not(mine))
            def _():
                q[zt, xt * hists + ht] = part
                copy2(zt, xt, ht).start()
        return carry

    lax.fori_loop(0, half, second, 0)
    hist_copy.start()

    def gather2(zt):
        def wait(o, carry):
            sl = lax.rem(slot + o, group)
            pltpu.make_async_remote_copy(
                src_ref=q.at[zt, sl], dst_ref=r2.at[zt, sl],
                send_sem=s2s.at[zt, sl], recv_sem=s2r.at[zt, sl],
                device_id=(space_id(z, sl // hists), lax.rem(sl, hists)), device_id_type=MESH,
            ).wait_recv()
            return carry

        lax.fori_loop(1, group, wait, 0)
        return jnp.sum(r2[zt].astype(jnp.float32), axis=0)

    def copy3(zt):
        return pltpu.make_async_remote_copy(
            src_ref=t3.at[zt], dst_ref=r3.at[z], send_sem=s3s.at[zt], recv_sem=s3r.at[z],
            device_id=(space_id(zt, x), h), device_id_type=MESH,
        )

    def third(zo, carry):
        zt = lax.rem(z + 1 + zo, z_size)
        t3[zt] = gather2(zt).astype(jnp.bfloat16)
        copy3(zt).start()
        return carry

    lax.fori_loop(0, z_size - 1, third, 0)
    far = gather2(z)

    inputs[3].wait()
    inputs[4].wait()
    inverse = 1.0 / self_ref[...]

    @pl.when(me == 0)
    def _():
        for n in range(SWEEPS - 1):
            halo[n, 0] = jnp.zeros((kh, width), jnp.bfloat16)

    @pl.when(me == space - 1)
    def _():
        for n in range(SWEEPS - 1):
            halo[n, 1] = jnp.zeros((kh, width), jnp.bfloat16)

    for o in range(1, z_size):
        zs = lax.rem(z + o, z_size)
        pltpu.make_async_remote_copy(
            src_ref=t3.at[zs], dst_ref=r3.at[zs], send_sem=s3s.at[zs], recv_sem=s3r.at[zs],
            device_id=(space_id(zs, x), h), device_id_type=MESH,
        ).wait_recv()
        far = far + r3[zs].astype(jnp.float32)
    near_copy.wait()
    right_side = exc_ref[...] - far
    current = right_side * inverse

    def edge(n, side):
        other = jnp.minimum(me + 1, space - 1) if side == 0 else jnp.maximum(me - 1, 0)
        return pltpu.make_async_remote_copy(
            src_ref=xs.at[n], dst_ref=halo.at[n, side],
            send_sem=xss.at[n, side], recv_sem=xsr.at[n, side],
            device_id=(other, h), device_id_type=MESH,
        )

    for n in range(SWEEPS - 1):
        rounded = current.astype(jnp.bfloat16)
        xs[n] = rounded

        @pl.when(me < space - 1)
        def _():
            edge(n, 0).start()

        @pl.when(me > 0)
        def _():
            edge(n, 1).start()

        product = lax.dot_general(rounded, nbuf[1], NT, preferred_element_type=jnp.float32)
        rest = right_side - product

        @pl.when(me > 0)
        def _():
            edge(n, 0).wait_recv()

        @pl.when(me < space - 1)
        def _():
            edge(n, 1).wait_recv()

        before = lax.dot_general(halo[n, 0], nbuf[0], NT, preferred_element_type=jnp.float32)
        after = lax.dot_general(halo[n, 1], nbuf[2], NT, preferred_element_type=jnp.float32)
        current = (rest - before - after) * inverse

    xlast[...] = current

    def give(o):
        ht = lax.rem(h + o, hists)
        return pltpu.make_async_remote_copy(
            src_ref=xlast, dst_ref=gath.at[h], send_sem=gs.at[ht], recv_sem=gr.at[h],
            device_id=(me, ht), device_id_type=MESH,
        )

    for o in range(1, hists):
        give(o).start()
    cur_out[h] = current
    hist_copy.wait()

    def drain(j, carry):
        zt, xt = chip_at(j)
        copy1(zt * x_size + xt).wait_send()
        for ht in range(hists):
            @pl.when(jnp.logical_not(jnp.logical_and(xt == x, h == ht)))
            def _():
                copy2(zt, xt, ht).wait_send()
        return carry

    lax.fori_loop(0, half, drain, 0)
    for o in range(1, z_size):
        copy3(lax.rem(z + o, z_size)).wait_send()

    @pl.when(me < space - 1)
    def _():
        for n in range(SWEEPS - 1):
            edge(n, 0).wait_send()

    @pl.when(me > 0)
    def _():
        for n in range(SWEEPS - 1):
            edge(n, 1).wait_send()

    for o in range(1, hists):
        hs_ = lax.rem(h + o, hists)
        pltpu.make_async_remote_copy(
            src_ref=xlast, dst_ref=gath.at[hs_], send_sem=gs.at[hs_], recv_sem=gr.at[hs_],
            device_id=(me, hs_), device_id_type=MESH,
        ).wait_recv()
        cur_out[hs_] = gath[hs_]
    out_cur = pltpu.make_async_copy(cur_out, cur_hbm, osem.at[0])
    out_cur.start()
    for o in range(1, hists):
        give(o).wait_send()

    @pl.when(h == 0)
    def _():
        newest[...] = cur_out[...].reshape(steps, width).astype(jnp.bfloat16)

    @pl.when(h > 0)
    def _():
        newest[...] = hin[...]

    out_hist = pltpu.make_async_copy(newest, hist_hbm_out.at[0], osem.at[1])
    out_hist.start()
    shift.wait()
    out_cur.wait()
    out_hist.wait()


def per_device(
    space, hists,
    history, right_factor, left_factor, pair_rank, pair_lag, near_block, self_term, excitation,
):
    lags, steps, width = history.shape
    pair_dev, rank_most, _ = right_factor.shape
    z_size, x_size, _ = shape_of(space)
    per = pair_dev // space
    kh = steps // hists
    half, group = space // 2, x_size * hists
    sweeps = SWEEPS - 1
    bf16 = jnp.bfloat16
    dma = pltpu.SemaphoreType.DMA
    hbm = pl.BlockSpec(memory_space=pltpu.HBM)
    flops = 2 * pair_dev * rank_most * width * steps * 2
    current, next_history = pl.pallas_call(
        functools.partial(kernel, (space, hists, z_size, x_size, per, rank_most)),
        out_shape=(
            jax.ShapeDtypeStruct((hists, kh, width), jnp.float32),
            jax.ShapeDtypeStruct((lags, steps, width), bf16),
        ),
        in_specs=[hbm] * 8,
        out_specs=(hbm, hbm),
        scratch_shapes=[
            pltpu.SMEM((pair_dev,), jnp.int32),
            pltpu.SMEM((pair_dev,), jnp.int32),
            pltpu.VMEM((lags, steps, width), bf16),
            pltpu.VMEM((1, width), jnp.float32),
            pltpu.VMEM((kh, width), jnp.float32),
            pltpu.VMEM((hists, kh, width), jnp.float32),
            pltpu.VMEM((steps, width), bf16),
            pltpu.VMEM((pair_dev, rank_most, width), bf16),
            pltpu.VMEM((pair_dev, rank_most, width), bf16),
            pltpu.VMEM(near_block.shape, bf16),
            pltpu.VMEM((half, steps, width), bf16),
            pltpu.VMEM((half, steps, width), bf16),
            pltpu.VMEM((z_size, group, kh, width), bf16),
            pltpu.VMEM((z_size, group, kh, width), bf16),
            pltpu.VMEM((z_size, kh, width), bf16),
            pltpu.VMEM((z_size, kh, width), bf16),
            pltpu.VMEM((sweeps, kh, width), bf16),
            pltpu.VMEM((sweeps, 2, kh, width), bf16),
            pltpu.VMEM((kh, width), jnp.float32),
            pltpu.VMEM((hists, kh, width), jnp.float32),
            pltpu.VMEM((steps, width), bf16),
            dma((space,)), dma((space,)), dma,
            dma((half,)), dma((half,)),
            dma((z_size, group)), dma((z_size, group)),
            dma((z_size,)), dma((z_size,)),
            dma((sweeps, 2)), dma((sweeps, 2)),
            dma((hists,)), dma((hists,)), dma((2,)), dma((5,)), dma((3,)),
        ],
        compiler_params=pltpu.CompilerParams(
            collective_id=0, has_side_effects=True, vmem_limit_bytes=64000 * 1024
        ),
        cost_estimate=pl.CostEstimate(
            flops=flops, bytes_accessed=4 * pair_dev * rank_most * width, transcendentals=0
        ),
    )(
        pair_lag.reshape(-1), pair_rank.reshape(-1), history, self_term.reshape(1, width),
        excitation.reshape(hists, kh, width), right_factor, left_factor, near_block,
    )
    return current.reshape(steps, width), next_history


def solution(mesh):
    in_specs = (
        P("hist", None, "space"),
        P("hist", None, "space"),
        P("hist", None, "space"),
        P("hist", "space"),
        P("hist", "space"),
        P(None, "space", None),
        P("space"),
        P(None, "space"),
    )
    out_specs = (P(None, "space"), P("hist", None, "space"))
    step = functools.partial(per_device, mesh.shape["space"], mesh.shape["hist"])
    return jax.shard_map(
        step, mesh=mesh, in_specs=in_specs, out_specs=out_specs, check_vma=False
    )
```

```python
import functools

import jax
import jax.numpy as jnp
from jax import lax
from jax.experimental import pallas as pl
from jax.experimental.pallas import tpu as pltpu
from jax.sharding import PartitionSpec as P

SWEEPS = 8
MESH = pl.DeviceIdType.MESH
NT = (((1,), (1,)), ((), ()))


def shape_of(space):
    cores = 2
    chips = space // cores
    z_size = 1
    while z_size * z_size * 4 <= space and chips % (z_size * 2) == 0:
        z_size *= 2
    return z_size, chips // z_size, cores


def kernel(
    dims,
    lag_hbm, rank_hbm, hist_hbm, self_hbm, exc_hbm, right_hbm, left_hbm, near_hbm,
    cur_hbm, newest_hbm,
    lag_ref, rank_ref, hist_ref, self_ref, exc_ref, cur_out, newest, rbuf, lbuf, nbuf, p1, r1, q, r2, t3, r3, xs, halo, xlast, gath, hin,
    rsem, lsem, nsem, s1s, s1r, s2s, s2r, s3s, s3r, xss, xsr, gs, gr, hs, isem, osem,
):
    space, hists, z_size, x_size, per, rank_most = dims
    lags, steps, width = hist_ref.shape
    kh = steps // hists
    parts, kg = xlast.shape[0], xlast.shape[1]
    me = lax.axis_index("space")
    h = lax.axis_index("hist")
    core = lax.rem(me, 2)
    chip = me // 2
    x = lax.rem(chip, x_size)
    z = chip // x_size
    mate = me + 1 - 2 * core
    half = space // 2
    group = x_size * hists
    slot = x * hists + h

    def chip_at(j):
        zo, xo = j // x_size, lax.rem(j, x_size)
        zt = lax.rem(z + 1 + zo, z_size)
        xt = lax.rem(x + 1 + xo, x_size)
        return zt, xt

    def load(t):
        rows = pl.ds(t * per, per)
        return (
            pltpu.make_async_copy(right_hbm.at[rows], rbuf.at[rows], rsem.at[t]),
            pltpu.make_async_copy(left_hbm.at[rows], lbuf.at[rows], lsem.at[t]),
        )

    def space_id(zt, xt):
        return (zt * x_size + xt) * 2 + core

    inputs = [
        pltpu.make_async_copy(a, b, isem.at[i])
        for i, (a, b) in enumerate((
            (hist_hbm, hist_ref), (lag_hbm, lag_ref), (rank_hbm, rank_ref),
            (exc_hbm.at[h], exc_ref), (self_hbm, self_ref),
        ))
    ]
    for c in inputs[:3]:
        c.start()

    barrier = pltpu.get_barrier_semaphore()

    def greet(s, hh):
        pl.semaphore_signal(barrier, inc=1, device_id=(s, hh), device_id_type=MESH)

    greet(mate, h)
    for o in range(1, group):
        sl = lax.rem(slot + o, group)
        greet(space_id(z, sl // hists), lax.rem(sl, hists))
    for o in range(1, z_size):
        greet(space_id(lax.rem(z + o, z_size), x), h)

    @pl.when(me > 0)
    def _():
        greet(me - 1, h)

    @pl.when(me < space - 1)
    def _():
        greet(me + 1, h)

    for side in range(2):
        def start(j, carry):
            zt, xt = chip_at(j)
            own = core if side else 1 - core
            for c in load((zt * x_size + xt) * 2 + own):
                c.start()
            return carry

        lax.fori_loop(0, half, start, 0)
    near_copy = pltpu.make_async_copy(near_hbm, nbuf, nsem)
    near_copy.start()
    inputs[3].start()
    inputs[4].start()

    for c in inputs[:3]:
        c.wait()
    hist_all = hist_ref[...].reshape(lags * steps, width)
    cols = lax.broadcasted_iota(jnp.int32, (1, per * rank_most), 1)

    def partial_of(t):
        for c in load(t):
            c.wait()
        rows = pl.ds(t * per, per)
        rr = rbuf[rows].reshape(per * rank_most, width)
        ll = lbuf[rows].reshape(per * rank_most, width)
        lag = jnp.full(cols.shape, lag_ref[t * per], jnp.int32)
        lim = jnp.full(cols.shape, rank_ref[t * per], jnp.int32)
        for i in range(1, per):
            at = cols >= i * rank_most
            lag = jnp.where(at, lag_ref[t * per + i], lag)
            lim = jnp.where(at, rank_ref[t * per + i] + i * rank_most, lim)
        lag = jnp.where(cols < lim, lag, lags)
        full = lax.dot_general(hist_all, rr, NT, preferred_element_type=jnp.float32)
        coef = jnp.zeros((steps, per * rank_most), jnp.float32)
        for g in range(lags):
            coef = jnp.where(lag == g, full[g * steps : (g + 1) * steps], coef)
        return jnp.dot(coef.astype(jnp.bfloat16), ll, preferred_element_type=jnp.float32)

    def copy1(b):
        return pltpu.make_async_remote_copy(
            src_ref=p1.at[b], dst_ref=r1.at[b], send_sem=s1s.at[b], recv_sem=s1r.at[b],
            device_id=(mate, h), device_id_type=MESH,
        )

    ends = jnp.minimum(me, 1) + jnp.minimum(space - 1 - me, 1)
    pl.semaphore_wait(barrier, 1 + (group - 1) + (z_size - 1) + ends)

    hist_copy = pltpu.make_async_remote_copy(
        src_ref=hist_ref.at[lags - 1], dst_ref=hin, send_sem=hs.at[0], recv_sem=hs.at[1],
        device_id=(me, lax.rem(h + 1, hists)), device_id_type=MESH,
    )

    def first(j, carry):
        zt, xt = chip_at(j)
        b = zt * x_size + xt
        p1[b] = partial_of(b * 2 + 1 - core).astype(jnp.bfloat16)
        copy1(b).start()
        return carry

    lax.fori_loop(0, half, first, 0)

    def copy2(zt, xt, ht):
        return pltpu.make_async_remote_copy(
            src_ref=q.at[zt, xt * hists + ht], dst_ref=r2.at[zt, slot],
            send_sem=s2s.at[zt, xt * hists + ht], recv_sem=s2r.at[zt, slot],
            device_id=(space_id(z, xt), ht), device_id_type=MESH,
        )

    def second(j, carry):
        zt, xt = chip_at(j)
        b = zt * x_size + xt
        value = partial_of(b * 2 + core)
        copy1(b).wait_recv()
        value = value + r1[b].astype(jnp.float32)
        low = value.astype(jnp.bfloat16)
        for ht in range(hists):
            part = low[ht * kh : (ht + 1) * kh]
            mine = jnp.logical_and(xt == x, h == ht)

            @pl.when(mine)
            def _():
                r2[zt, slot] = part

            @pl.when(jnp.logical_not(mine))
            def _():
                q[zt, xt * hists + ht] = part
                copy2(zt, xt, ht).start()
        return carry

    lax.fori_loop(0, half, second, 0)
    hist_copy.start()

    def gather2(zt):
        def wait(o, carry):
            sl = lax.rem(slot + o, group)
            pltpu.make_async_remote_copy(
                src_ref=q.at[zt, sl], dst_ref=r2.at[zt, sl],
                send_sem=s2s.at[zt, sl], recv_sem=s2r.at[zt, sl],
                device_id=(space_id(z, sl // hists), lax.rem(sl, hists)), device_id_type=MESH,
            ).wait_recv()
            return carry

        lax.fori_loop(1, group, wait, 0)
        return jnp.sum(r2[zt].astype(jnp.float32), axis=0)

    def copy3(zt):
        return pltpu.make_async_remote_copy(
            src_ref=t3.at[zt], dst_ref=r3.at[z], send_sem=s3s.at[zt], recv_sem=s3r.at[z],
            device_id=(space_id(zt, x), h), device_id_type=MESH,
        )

    def third(zo, carry):
        zt = lax.rem(z + 1 + zo, z_size)
        t3[zt] = gather2(zt).astype(jnp.bfloat16)
        copy3(zt).start()
        return carry

    lax.fori_loop(0, z_size - 1, third, 0)
    far = gather2(z)

    inputs[3].wait()
    inputs[4].wait()
    inverse = 1.0 / self_ref[...]

    @pl.when(me == 0)
    def _():
        for n in range(SWEEPS - 1):
            halo[n, 0] = jnp.zeros((parts, kg, width), jnp.bfloat16)

    @pl.when(me == space - 1)
    def _():
        for n in range(SWEEPS - 1):
            halo[n, 1] = jnp.zeros((parts, kg, width), jnp.bfloat16)

    for o in range(1, z_size):
        zs = lax.rem(z + o, z_size)
        pltpu.make_async_remote_copy(
            src_ref=t3.at[zs], dst_ref=r3.at[zs], send_sem=s3s.at[zs], recv_sem=s3r.at[zs],
            device_id=(space_id(zs, x), h), device_id_type=MESH,
        ).wait_recv()
        far = far + r3[zs].astype(jnp.float32)
    near_copy.wait()
    right_side = exc_ref[...] - far
    right_part = [right_side[g * kg : (g + 1) * kg] for g in range(parts)]
    current = [r * inverse for r in right_part]
    rest = [None] * parts

    def edge(n, g, side):
        other = jnp.minimum(me + 1, space - 1) if side == 0 else jnp.maximum(me - 1, 0)
        i = n * parts + g
        return pltpu.make_async_remote_copy(
            src_ref=xs.at[n, g], dst_ref=halo.at[n, side, g],
            send_sem=xss.at[i, side], recv_sem=xsr.at[i, side],
            device_id=(other, h), device_id_type=MESH,
        )

    def begin(n, g):
        rounded = current[g].astype(jnp.bfloat16)
        xs[n, g] = rounded

        @pl.when(me < space - 1)
        def _():
            edge(n, g, 0).start()

        @pl.when(me > 0)
        def _():
            edge(n, g, 1).start()

        product = lax.dot_general(rounded, nbuf[1], NT, preferred_element_type=jnp.float32)
        rest[g] = right_part[g] - product

    def give(o, g):
        ht = lax.rem(h + o, hists)
        return pltpu.make_async_remote_copy(
            src_ref=xlast.at[g], dst_ref=gath.at[h, g],
            send_sem=gs.at[g, ht], recv_sem=gr.at[g, h],
            device_id=(me, ht), device_id_type=MESH,
        )

    for g in range(parts):
        begin(0, g)
    for n in range(SWEEPS - 1):
        for g in range(parts):
            @pl.when(me > 0)
            def _():
                edge(n, g, 0).wait_recv()

            @pl.when(me < space - 1)
            def _():
                edge(n, g, 1).wait_recv()

            before = lax.dot_general(
                halo[n, 0, g], nbuf[0], NT, preferred_element_type=jnp.float32
            )
            after = lax.dot_general(
                halo[n, 1, g], nbuf[2], NT, preferred_element_type=jnp.float32
            )
            current[g] = (rest[g] - before - after) * inverse
            if n < SWEEPS - 2:
                begin(n + 1, g)
            else:
                xlast[g] = current[g].astype(jnp.bfloat16)
                for o in range(1, hists):
                    give(o, g).start()
                cur_out[h, g] = current[g]
    hist_copy.wait()

    def drain(j, carry):
        zt, xt = chip_at(j)
        copy1(zt * x_size + xt).wait_send()
        for ht in range(hists):
            @pl.when(jnp.logical_not(jnp.logical_and(xt == x, h == ht)))
            def _():
                copy2(zt, xt, ht).wait_send()
        return carry

    lax.fori_loop(0, half, drain, 0)
    for o in range(1, z_size):
        copy3(lax.rem(z + o, z_size)).wait_send()

    @pl.when(me < space - 1)
    def _():
        for n in range(SWEEPS - 1):
            for g in range(parts):
                edge(n, g, 0).wait_send()

    @pl.when(me > 0)
    def _():
        for n in range(SWEEPS - 1):
            for g in range(parts):
                edge(n, g, 1).wait_send()

    for g in range(parts):
        for o in range(1, hists):
            hs_ = lax.rem(h + o, hists)
            pltpu.make_async_remote_copy(
                src_ref=xlast.at[g], dst_ref=gath.at[hs_, g],
                send_sem=gs.at[g, hs_], recv_sem=gr.at[g, hs_],
                device_id=(me, hs_), device_id_type=MESH,
            ).wait_recv()
            cur_out[hs_, g] = gath[hs_, g].astype(jnp.float32)
    out_cur = pltpu.make_async_copy(cur_out, cur_hbm, osem.at[0])
    out_cur.start()
    for o in range(1, hists):
        for g in range(parts):
            give(o, g).wait_send()

    @pl.when(h == 0)
    def _():
        newest[...] = cur_out[...].reshape(steps, width).astype(jnp.bfloat16)

    @pl.when(h > 0)
    def _():
        newest[...] = hin[...]

    out_hist = pltpu.make_async_copy(newest, newest_hbm, osem.at[1])
    out_hist.start()
    out_cur.wait()
    out_hist.wait()


def finish(current, newest, history, current_out, history_out, cbuf, hbuf, isem, osem):
    lags = history.shape[0]
    older = pl.ds(1, lags - 1)
    come = [
        pltpu.make_async_copy(current, cbuf, isem.at[0]),
        pltpu.make_async_copy(newest, hbuf.at[0], isem.at[1]),
        pltpu.make_async_copy(history.at[pl.ds(0, lags - 1)], hbuf.at[older], isem.at[2]),
    ]
    go = [
        pltpu.make_async_copy(cbuf, current_out, osem.at[0]),
        pltpu.make_async_copy(hbuf.at[0], history_out.at[0], osem.at[1]),
        pltpu.make_async_copy(hbuf.at[older], history_out.at[older], osem.at[2]),
    ]
    for c in come:
        c.start()
    for c, d in zip(come, go):
        c.wait()
        d.start()
    for d in go:
        d.wait()


def per_device(
    space, hists,
    history, right_factor, left_factor, pair_rank, pair_lag, near_block, self_term, excitation,
):
    lags, steps, width = history.shape
    pair_dev, rank_most, _ = right_factor.shape
    z_size, x_size, _ = shape_of(space)
    per = pair_dev // space
    kh = steps // hists
    parts = 2 if kh % 32 == 0 else 1
    kg = kh // parts
    half, group = space // 2, x_size * hists
    sweeps = SWEEPS - 1
    bf16 = jnp.bfloat16
    dma = pltpu.SemaphoreType.DMA
    hbm = pl.BlockSpec(memory_space=pltpu.HBM)
    flops = 2 * pair_dev * rank_most * width * steps * 2
    current, newest = pl.pallas_call(
        functools.partial(kernel, (space, hists, z_size, x_size, per, rank_most)),
        out_shape=(
            jax.ShapeDtypeStruct((hists, parts, kg, width), jnp.float32),
            jax.ShapeDtypeStruct((steps, width), bf16),
        ),
        in_specs=[hbm] * 8,
        out_specs=(hbm, hbm),
        scratch_shapes=[
            pltpu.SMEM((pair_dev,), jnp.int32),
            pltpu.SMEM((pair_dev,), jnp.int32),
            pltpu.VMEM((lags, steps, width), bf16),
            pltpu.VMEM((1, width), jnp.float32),
            pltpu.VMEM((kh, width), jnp.float32),
            pltpu.VMEM((hists, parts, kg, width), jnp.float32),
            pltpu.VMEM((steps, width), bf16),
            pltpu.VMEM((pair_dev, rank_most, width), bf16),
            pltpu.VMEM((pair_dev, rank_most, width), bf16),
            pltpu.VMEM(near_block.shape, bf16),
            pltpu.VMEM((half, steps, width), bf16),
            pltpu.VMEM((half, steps, width), bf16),
            pltpu.VMEM((z_size, group, kh, width), bf16),
            pltpu.VMEM((z_size, group, kh, width), bf16),
            pltpu.VMEM((z_size, kh, width), bf16),
            pltpu.VMEM((z_size, kh, width), bf16),
            pltpu.VMEM((sweeps, parts, kg, width), bf16),
            pltpu.VMEM((sweeps, 2, parts, kg, width), bf16),
            pltpu.VMEM((parts, kg, width), bf16),
            pltpu.VMEM((hists, parts, kg, width), bf16),
            pltpu.VMEM((steps, width), bf16),
            dma((space,)), dma((space,)), dma,
            dma((half,)), dma((half,)),
            dma((z_size, group)), dma((z_size, group)),
            dma((z_size,)), dma((z_size,)),
            dma((sweeps * parts, 2)), dma((sweeps * parts, 2)),
            dma((parts, hists)), dma((parts, hists)), dma((2,)), dma((5,)), dma((2,)),
        ],
        compiler_params=pltpu.CompilerParams(
            collective_id=0, has_side_effects=True, vmem_limit_bytes=64000 * 1024
        ),
        cost_estimate=pl.CostEstimate(
            flops=flops, bytes_accessed=4 * pair_dev * rank_most * width, transcendentals=0
        ),
    )(
        pair_lag.reshape(-1), pair_rank.reshape(-1), history, self_term.reshape(1, width),
        excitation.reshape(hists, kh, width), right_factor, left_factor, near_block,
    )
    return pl.pallas_call(
        finish,
        out_shape=(
            jax.ShapeDtypeStruct((steps, width), jnp.float32),
            jax.ShapeDtypeStruct((lags, steps, width), bf16),
        ),
        in_specs=[hbm] * 3,
        out_specs=(hbm, hbm),
        scratch_shapes=[
            pltpu.VMEM((steps, width), jnp.float32),
            pltpu.VMEM((lags, steps, width), bf16),
            dma((3,)), dma((3,)),
        ],
        compiler_params=pltpu.CompilerParams(vmem_limit_bytes=64000 * 1024),
    )(current.reshape(steps, width), newest, history)


def solution(mesh):
    in_specs = (
        P("hist", None, "space"),
        P("hist", None, "space"),
        P("hist", None, "space"),
        P("hist", "space"),
        P("hist", "space"),
        P(None, "space", None),
        P("space"),
        P(None, "space"),
    )
    out_specs = (P(None, "space"), P("hist", None, "space"))
    step = functools.partial(per_device, mesh.shape["space"], mesh.shape["hist"])
    return jax.shard_map(
        step, mesh=mesh, in_specs=in_specs, out_specs=out_specs, check_vma=False
    )
```
